32 devices in a mesh: dp: 8 (over z, core), ctx: 4 (over y, x).
Axes of the slice: x: 2, y: 2, z: 4, core: 2. Of those that a mesh axis runs over, the one named last changes fastest.
Arguments:
- queries: bfloat16 [8, 1536, 1024], P('dp', 'ctx'), may hold values from -32 to 32
- keys: bfloat16 [8, 1536, 1024], P('dp', 'ctx'), may hold values from -32 to 32
- values: bfloat16 [8, 1536, 1024], P('dp', 'ctx'), may hold values from -6 to 6
- out_weight: bfloat16 [2048, 1024], replicated, may hold values from -0.1875 to 0.1875
- out_cot: bfloat16 [8, 1536, 2048], P('dp', 'ctx'), may hold values from -6 to 6
- block_list: int32 [12, 8], replicated, may hold values from 0 to 11, as said below
Outputs:
- attended: bfloat16 [8, 1536, 2048], P('dp', 'ctx')
- query_gradient: bfloat16 [8, 1536, 1024], P('dp', 'ctx')
- key_grad: bfloat16 [8, 1536, 1024], P('dp', 'ctx')
- value_grad: bfloat16 [8, 1536, 1024], P('dp', 'ctx')
- weight_grad: float32 [2048, 1024], P(('dp', 'ctx'))
The draws below stay inside these ranges and needn't reach their ends.
Inputs may be any that keep to these rules, and one draw needn't show every extreme that they name: `block_list`: row i names 8 different blocks: i - 1, i and i + 1 modulo 12, then the 2 global blocks (the same in every row) where they are not among those three, then other blocks at random.
All inputs are finite; a program needn't handle non-finite values.
Results may differ from the reference program's by a relative error of at most 0.015.
Values may be sent and summed in bfloat16 or wider, within the bound.
A program may use at most 128 MiB of HBM per device.

```python
import math
import jax
import jax.numpy as jnp
from jax import lax

D = 2048
HEADS = 8
HEAD_SIZE = 128
BLOCK_TOKENS = 128
CHOSEN_BLOCKS = 8
NGLOB = 2
HD = 1024
SEQ = 1536
NBLK = 12
N_DP = 8


def drawn_pair(key):
    full_shape = (N_DP, SEQ, HD)
    base_query = jax.random.normal(jax.random.fold_in(key, 11), full_shape, jnp.float32)
    base_key = jax.random.normal(jax.random.fold_in(key, 12), full_shape, jnp.float32)
    return (1.4 * jnp.clip(base_query, -6.0, 6.0), 1.4 * jnp.clip(base_key, -6.0, 6.0))


def draw_queries(key, part):
    return drawn_pair(key)[0].astype(jnp.bfloat16)


def draw_keys(key, part):
    return drawn_pair(key)[1].astype(jnp.bfloat16)


def draw_block_list(key, part):
    rows_idx = jnp.arange(NBLK, dtype=jnp.int32)[:, None]
    cols_idx = jnp.arange(NBLK, dtype=jnp.int32)[None, :]
    glob_score = jax.random.randint(jax.random.fold_in(key, 21), (NBLK,), 0, 1 << 16, dtype=jnp.int32) * NBLK + jnp.arange(NBLK, dtype=jnp.int32)
    unused_vals, global_ids = lax.top_k(glob_score, NGLOB)
    is_global = jnp.any(jnp.arange(NBLK, dtype=jnp.int32)[:, None] == global_ids[None, :], axis=1).astype(jnp.int32)
    priority = jax.random.randint(jax.random.fold_in(key, 22), (NBLK, NBLK), 0, 1 << 12, dtype=jnp.int32) * NBLK + cols_idx + is_global[None, :] * (1 << 22)
    offset = (cols_idx - rows_idx) % NBLK
    in_window = (offset == 0) | (offset == 1) | (offset == NBLK - 1)
    priority = jnp.where(in_window, -1, priority)
    unused_top, picked = lax.top_k(priority, CHOSEN_BLOCKS - 3)
    window = jnp.concatenate([(rows_idx - 1) % NBLK, rows_idx, (rows_idx + 1) % NBLK], axis=1)
    return jnp.concatenate([window, picked.astype(jnp.int32)], axis=1).astype(jnp.int32)


def levels(stream_key, dims, shards, low, high):
    factor_of, own = 1.0, jax.random.fold_in(stream_key, 6)
    for dim, parts in shards:
        draws = jnp.exp(jax.random.uniform(jax.random.fold_in(own, dim), (parts,), jnp.float32, low / len(shards), high / len(shards)))
        factor_of = factor_of * jnp.repeat(draws, dims[dim] // parts).reshape([-1 if axis == dim else 1 for axis in range(len(dims))])
    return factor_of


def normal_values(own_key, dims, spread, reach, pieces=(), held_as=jnp.bfloat16):
    result = jax.random.normal(own_key, dims, jnp.float32) * spread
    if len(pieces) > 0:
        result = levels(own_key, dims, pieces, -0.22, 0.18) * result
    return jnp.clip(result, min=-reach, max=reach).astype(held_as)


def setup_inputs(seed: int = 0) -> dict:
    arg_keys = jax.random.split(jax.random.key(seed), 7)
    queries = draw_queries(jax.random.fold_in(arg_keys[6], 71), 0)
    keys = draw_keys(jax.random.fold_in(arg_keys[6], 71), 0)
    values = normal_values(arg_keys[2], (N_DP, SEQ, HD), 1.0, 6.0, ((0, 8), (1, 4)))
    out_weight = normal_values(arg_keys[3], (D, HD), HD ** -0.5, 0.1875)
    out_cot = normal_values(arg_keys[4], (N_DP, SEQ, D), 1.0, 6.0, ((0, 8), (1, 4)))
    block_list = draw_block_list(jax.random.fold_in(arg_keys[6], 71), 0)
    return {"queries": queries, "keys": keys, "values": values, "out_weight": out_weight, "out_cot": out_cot, "block_list": block_list}


def select_rows(source_table, block_list):
    block_total = block_list.shape[0]
    gathered = source_table[block_list.reshape(-1)]
    return gathered.reshape(block_total, CHOSEN_BLOCKS * BLOCK_TOKENS, HEAD_SIZE)

def head_pass(query_head, key_head, value_head, cot_head, block_list):
    block_total = block_list.shape[0]
    inverse_root_scale = 1.0 / math.sqrt(HEAD_SIZE)
    blocked_queries = query_head.reshape(block_total, BLOCK_TOKENS, HEAD_SIZE).astype(jnp.float32)
    chosen_keys = select_rows(key_head.reshape(block_total, BLOCK_TOKENS, HEAD_SIZE), block_list).astype(jnp.float32)
    chosen_values = select_rows(value_head.reshape(block_total, BLOCK_TOKENS, HEAD_SIZE), block_list).astype(jnp.float32)
    logit_scores = jnp.einsum('vht,vrt->vhr', blocked_queries, chosen_keys) * inverse_root_scale
    row_max = lax.optimization_barrier(jnp.max(logit_scores, axis=-1, keepdims=True))
    expo_rows = jnp.exp(logit_scores - row_max)
    row_sum = lax.optimization_barrier(jnp.sum(expo_rows, axis=-1, keepdims=True))
    log_total = row_max + jnp.log(row_sum)
    weight_matrix = (expo_rows / row_sum).astype(jnp.bfloat16)
    attention_probs = jnp.einsum('ysl,yli->ysi', weight_matrix.astype(jnp.float32), chosen_values).astype(jnp.bfloat16)
    cotangent_block_rows = cot_head.reshape(block_total, BLOCK_TOKENS, HEAD_SIZE).astype(jnp.float32)
    row_dot = lax.optimization_barrier(jnp.sum(cotangent_block_rows * attention_probs.astype(jnp.float32), axis=-1))
    probs = jnp.exp(logit_scores - log_total)
    probs_narrow = probs.astype(jnp.bfloat16).astype(jnp.float32)
    flat_picks = block_list.reshape(-1).astype(jnp.int32)
    value_grad_terms = jnp.einsum('lgh,lga->lha', probs_narrow, cotangent_block_rows).reshape(block_total * CHOSEN_BLOCKS, BLOCK_TOKENS, HEAD_SIZE)
    value_acc = jnp.zeros((block_total, BLOCK_TOKENS, HEAD_SIZE), jnp.float32).at[flat_picks].add(value_grad_terms)
    cotangent_probs = jnp.einsum('vht,vrt->vhr', cotangent_block_rows, chosen_values)
    score_cotangent = (probs * (cotangent_probs - row_dot[..., None])).astype(jnp.bfloat16).astype(jnp.float32)
    query_gradient = (jnp.einsum('ysl,yli->ysi', score_cotangent, chosen_keys) * inverse_root_scale).astype(jnp.bfloat16)
    key_grad_terms = jnp.einsum('lgh,lga->lha', score_cotangent, blocked_queries).reshape(block_total * CHOSEN_BLOCKS, BLOCK_TOKENS, HEAD_SIZE)
    key_acc = jnp.zeros((block_total, BLOCK_TOKENS, HEAD_SIZE), jnp.float32).at[flat_picks].add(key_grad_terms)
    key_grad = (key_acc * inverse_root_scale).astype(jnp.bfloat16)
    value_grad = value_acc.astype(jnp.bfloat16)
    return (attention_probs.reshape(SEQ, HEAD_SIZE), query_gradient.reshape(SEQ, HEAD_SIZE), key_grad.reshape(SEQ, HEAD_SIZE), value_grad.reshape(SEQ, HEAD_SIZE))

def split_heads(matrix):
    return matrix.reshape(SEQ, HEADS, HEAD_SIZE).transpose(1, 0, 2)

def join_heads(stacked):
    return stacked.transpose(1, 0, 2).reshape(SEQ, HD)

def reference(queries, keys, values, out_weight, out_cot, block_list):

    def replica(running, inputs):
        query_rows, key_rows, value_rows, cot_rows = inputs
        attn_cot = jnp.dot(cot_rows, out_weight, preferred_element_type=jnp.float32).astype(jnp.bfloat16)

        def one_head(packed):
            return head_pass(packed[0], packed[1], packed[2], packed[3], block_list)
        results = lax.map(one_head, (split_heads(query_rows), split_heads(key_rows), split_heads(value_rows), split_heads(attn_cot)))
        attention_probs = join_heads(results[0])
        attended = jnp.dot(attention_probs, out_weight.T, preferred_element_type=jnp.float32).astype(jnp.bfloat16)
        weight_term = jnp.dot(cot_rows.T, attention_probs, preferred_element_type=jnp.float32)
        outputs = (attended, join_heads(results[1]), join_heads(results[2]), join_heads(results[3]))
        return (running + weight_term, outputs)
    start_sum = jnp.zeros((D, HD), jnp.float32)
    weight_sum, stacked = lax.scan(replica, start_sum, (queries, keys, values, out_cot))
    weight_grad = weight_sum / N_DP
    return (stacked[0], stacked[1], stacked[2], stacked[3], weight_grad)
```

```python
import functools
import math

import jax
import jax.numpy as jnp
from jax import lax
from jax.experimental import pallas as pl
from jax.experimental.pallas import tpu as pltpu
from jax.sharding import PartitionSpec as P

HEAD_SIZE = 128
BLOCK_TOKENS = 128
MESH = pl.DeviceIdType.MESH
BF16 = jnp.bfloat16
F32 = jnp.float32
VMEM_BYTES = 56 * 1024 * 1024


def mm(a, b, ca=1, cb=0):
    return lax.dot_general(a, b, (((ca,), (cb,)), ((), ())), preferred_element_type=F32)


def gather_kernel(
    n, q, k, v, w, oc, qo, ko, vo, co, oct_, wv, ocv, cotbuf, octv, send, recv, loc
):
    me = lax.axis_index("ctx")
    dp = lax.axis_index("dp")
    tokens = q.shape[0]
    hc = qo.shape[1]
    barrier = pltpu.get_barrier_semaphore()
    for d in range(1, n):
        pl.semaphore_signal(
            barrier, inc=1, device_id=(dp, lax.rem(me + d, n)), device_id_type=MESH
        )
    load_oc = pltpu.make_async_copy(oc, ocv, loc.at[0])
    load_oc.start()
    load_w = pltpu.make_async_copy(w, wv, loc.at[1])
    load_w.start()
    pl.semaphore_wait(barrier, n - 1)
    mine = pl.ds(pl.multiple_of(me * tokens, tokens), tokens)

    def cols(p):
        return pl.ds(pl.multiple_of(p * hc, hc), hc)

    remote, local = [], []
    for t, (src, dst) in enumerate(((q, qo), (k, ko), (v, vo))):
        for d in range(1, n):
            p = lax.rem(me + d, n)
            copy = pltpu.make_async_remote_copy(
                src.at[:, cols(p)], dst.at[mine, :], send.at[t, d], recv.at[t, d],
                device_id=(dp, p), device_id_type=MESH,
            )
            copy.start()
            remote.append(copy)
        copy = pltpu.make_async_copy(src.at[:, cols(me)], dst.at[mine, :], loc.at[2 + t])
        copy.start()
        local.append(copy)
    load_oc.wait()
    load_w.wait()
    for d in list(range(1, n)) + [0]:
        p = lax.rem(me + d, n)
        cotbuf[d] = mm(ocv[...], wv[:, cols(p)]).astype(BF16)
        if d:
            copy = pltpu.make_async_remote_copy(
                cotbuf.at[d], co.at[mine, :], send.at[3, d], recv.at[3, d],
                device_id=(dp, p), device_id_type=MESH,
            )
            remote.append(copy)
        else:
            copy = pltpu.make_async_copy(cotbuf.at[0], co.at[mine, :], loc.at[5])
            local.append(copy)
        copy.start()
    width = 256

    def flip(i, carry):
        at = pl.ds(pl.multiple_of(i * width, width), width)
        octv[at, :] = ocv[:, at].T
        return carry

    lax.fori_loop(0, oc.shape[1] // width, flip, 0)
    copy = pltpu.make_async_copy(octv, oct_, loc.at[6])
    copy.start()
    local.append(copy)
    for copy in local:
        copy.wait()
    for copy in remote:
        copy.wait()


def attention_kernel(heads, chosen, scale, picks, q, c, k, v, attn, dq, dk, dv, kt, vt, ka, va):
    step = pl.program_id(0)
    blocks = pl.num_programs(0)

    def rows(b):
        return pl.ds(pl.multiple_of(b * BLOCK_TOKENS, BLOCK_TOKENS), BLOCK_TOKENS)

    @pl.when(step == 0)
    def _():
        ka[...] = jnp.zeros_like(ka)
        va[...] = jnp.zeros_like(va)

        def turn(b, carry):
            for h in range(heads):
                hs = slice(h * HEAD_SIZE, (h + 1) * HEAD_SIZE)
                kt[h, b] = k[rows(b), hs].T
                vt[h, b] = v[rows(b), hs].T
            return carry

        lax.fori_loop(0, k.shape[0] // BLOCK_TOKENS, turn, 0)

    names = [picks[step, j] for j in range(chosen)]
    factor = scale * math.log2(math.e)
    for h in range(heads):
        hs = slice(h * HEAD_SIZE, (h + 1) * HEAD_SIZE)
        qh = q[:, hs]
        ch = c[:, hs]
        ks = jnp.concatenate([k[rows(b), hs] for b in names], axis=0)
        vs = jnp.concatenate([v[rows(b), hs] for b in names], axis=0)
        kts = jnp.concatenate([kt[h, b] for b in names], axis=1)
        vts = jnp.concatenate([vt[h, b] for b in names], axis=1)
        st = mm(ks, qh, 1, 1)
        top = jnp.max(st, axis=0, keepdims=True)
        e = jnp.exp2((st - top) * factor)
        inv = 1.0 / jnp.sum(e, axis=0, keepdims=True)
        pt = e * inv
        low = pt.astype(BF16)
        at = mm(vts, low).astype(BF16)
        a = at.T
        attn[:, hs] = a
        dot = jnp.sum(ch.astype(F32).T * at.astype(F32), axis=0, keepdims=True)
        dpt = mm(vs, ch, 1, 1)
        ds = (pt * (dpt - dot)).astype(BF16)
        dq[:, hs] = (mm(kts, ds) * scale).T.astype(BF16)
        dks = mm(ds, qh)
        dvs = mm(low, ch)
        for j, b in enumerate(names):
            part = slice(j * BLOCK_TOKENS, (j + 1) * BLOCK_TOKENS)
            ka[h, b] += dks[part]
            va[h, b] += dvs[part]

    @pl.when(step == blocks - 1)
    def _():
        def put(b, carry):
            for h in range(heads):
                hs = slice(h * HEAD_SIZE, (h + 1) * HEAD_SIZE)
                dk[rows(b), hs] = (ka[h, b] * scale).astype(BF16)
                dv[rows(b), hs] = va[h, b].astype(BF16)
            return carry

        lax.fori_loop(0, k.shape[0] // BLOCK_TOKENS, put, 0)


def scatter_kernel(
    n, nz, attn, dq, dk, dv, w, oct_, out, dqo, dko, dvo, wg,
    seq, wv, octv, acc, csend, crecv, zsend, rrecv, lrecv, xsend, xrecv,
    send, recv, loc, csem_s, csem_r, zsem_s, rsem_r, lsem_r, xsem_s, xsem_r,
):
    me = lax.axis_index("ctx")
    dp = lax.axis_index("dp")
    core = lax.rem(dp, 2)
    other = dp + 1 - 2 * core
    z = dp // 2
    tokens, total = seq.shape
    hc = attn.shape[1]
    sub = wg.shape[0]
    barrier = pltpu.get_barrier_semaphore()
    up = lax.rem(z + 1, nz) * 2 + core
    down = lax.rem(z + nz - 1, nz) * 2 + core
    for d in range(1, n):
        pl.semaphore_signal(
            barrier, inc=1, device_id=(dp, lax.rem(me + d, n)), device_id_type=MESH
        )
    for target in (other, up, down):
        pl.semaphore_signal(barrier, inc=1, device_id=(target, me), device_id_type=MESH)
    load_oct = pltpu.make_async_copy(oct_, octv, loc.at[0])
    load_oct.start()
    load_w = pltpu.make_async_copy(w, wv, loc.at[1])
    load_w.start()
    pl.semaphore_wait(barrier, n - 1 + 3)

    def rows(p):
        return pl.ds(pl.multiple_of(p * tokens, tokens), tokens)

    mycols = pl.ds(pl.multiple_of(me * hc, hc), hc)

    def spread(t, src, dst):
        remote = []
        for d in range(1, n):
            p = lax.rem(me + d, n)
            copy = pltpu.make_async_remote_copy(
                src.at[rows(p), :], dst.at[:, mycols], send.at[t, d], recv.at[t, d],
                device_id=(dp, p), device_id_type=MESH,
            )
            copy.start()
            remote.append(copy)
        own = pltpu.make_async_copy(src.at[rows(me), :], dst.at[:, mycols], loc.at[2 + t])
        own.start()
        return own, remote

    own, remote = spread(0, attn, seq)
    own.wait()
    for copy in remote:
        copy.wait_recv()
    grads = [spread(1 + t, s, o) for t, (s, o) in enumerate(((dq, dqo), (dk, dko), (dv, dvo)))]
    load_oct.wait()
    load_w.wait()

    def term(c, s, who):
        base = pl.multiple_of(((2 * c + who) * n + s) * sub, sub)
        return mm(octv[pl.ds(base, sub), :], seq[...])

    def core_copy(c):
        return pltpu.make_async_remote_copy(
            csend.at[c], crecv.at[c], csem_s.at[c], csem_r.at[c],
            device_id=(other, me), device_id_type=MESH,
        )

    def give(c, carry):
        for s in range(n):
            csend[c, s] = term(c, s, 1 - core).astype(BF16)
        core_copy(c).start()
        return carry

    lax.fori_loop(0, nz, give, 0)

    def keep(c, carry):
        for s in range(n):
            acc[c, s] = term(c, s, core)
        return carry

    lax.fori_loop(0, nz, keep, 0)

    def take(c, carry):
        core_copy(c).wait()
        for s in range(n):
            acc[c, s] += crecv[c, s].astype(F32)
        return carry

    lax.fori_loop(0, nz, take, 0)

    def right(c, s):
        return pltpu.make_async_remote_copy(
            zsend.at[c, s], rrecv.at[c, s], zsem_s.at[c, s], rsem_r.at[c, s],
            device_id=(up, me), device_id_type=MESH,
        )

    def left(c, s):
        return pltpu.make_async_remote_copy(
            zsend.at[c, s], lrecv.at[c, s], zsem_s.at[c, s], lsem_r.at[c, s],
            device_id=(down, me), device_id_type=MESH,
        )

    def line(u, carry):
        i = u - z

        @pl.when((i >= 0) & (i < (nz - 1 - z) * n))
        def _():
            c = nz - 1 - i // n
            s = lax.rem(i, n)

            @pl.when(z > 0)
            def _():
                right(c, s).wait_recv()
                acc[c, s] += rrecv[c, s].astype(F32)

            zsend[c, s] = acc[c, s].astype(BF16)
            right(c, s).start()

        j = u - (nz - 1 - z)

        @pl.when((j >= 0) & (j < z * n))
        def _():
            c = j // n
            s = lax.rem(j, n)

            @pl.when(z < nz - 1)
            def _():
                left(c, s).wait_recv()
                acc[c, s] += lrecv[c, s].astype(F32)

            zsend[c, s] = acc[c, s].astype(BF16)
            left(c, s).start()

        @pl.when(u < tiles)
        def _():
            at = pl.ds(pl.multiple_of(u * tile, tile), tile)
            out[:, at] = mm(seq[...], wv[at, :], 1, 1).astype(BF16)

        return carry

    tile = 256
    tiles = wv.shape[0] // tile
    lax.fori_loop(0, max((nz - 1) * n + nz, tiles), line, 0)

    def cross(s, slot):
        return pltpu.make_async_remote_copy(
            xsend.at[s], xrecv.at[slot], xsem_s.at[s], xsem_r.at[slot],
            device_id=(dp, s), device_id_type=MESH,
        )

    def finish(s, carry):
        @pl.when(z > 0)
        def _():
            right(z, s).wait_recv()
            acc[z, s] += rrecv[z, s].astype(F32)

        @pl.when(z < nz - 1)
        def _():
            left(z, s).wait_recv()
            acc[z, s] += lrecv[z, s].astype(F32)

        @pl.when(s != me)
        def _():
            xsend[s] = acc[z, s].astype(BF16)
            cross(s, me).start()

        return carry

    lax.fori_loop(0, n, finish, 0)
    wg[...] = acc[z, me]

    def gather(p, carry):
        @pl.when(p != me)
        def _():
            cross(p, p).wait_recv()
            wg[...] += xrecv[p].astype(F32)

        return carry

    lax.fori_loop(0, n, gather, 0)
    wg[...] = wg[...] * (1.0 / (2 * nz))

    def drain(s, carry):
        @pl.when(s != me)
        def _():
            cross(s, me).wait_send()

        for c in range(nz):
            @pl.when(z < c)
            def _():
                right(c, s).wait_send()

            @pl.when(z > c)
            def _():
                left(c, s).wait_send()

        return carry

    lax.fori_loop(0, n, drain, 0)
    for copy in remote:
        copy.wait_send()
    for own, copies in grads:
        own.wait()
        for copy in copies:
            copy.wait()


def shards(queries, keys, values, out_weight, out_cot, block_list):
    n = lax.axis_size("ctx")
    n_dp = lax.axis_size("dp")
    nz = n_dp // 2
    _, tokens, total = queries.shape
    model = out_weight.shape[0]
    hc = total // n
    heads = hc // HEAD_SIZE
    length = tokens * n
    blocks = length // BLOCK_TOKENS
    chosen = block_list.shape[1]
    sub = model // (n * n_dp)
    anyspec = pl.BlockSpec(memory_space=pl.ANY)
    vspec = pl.BlockSpec(memory_space=pltpu.VMEM)
    dma = pltpu.SemaphoreType.DMA

    byhead = jax.ShapeDtypeStruct((length, hc), BF16)
    bytoken = jax.ShapeDtypeStruct((tokens, total), BF16)
    qh, kh, vh, ch, oct_ = pl.pallas_call(
        functools.partial(gather_kernel, n),
        out_shape=(byhead, byhead, byhead, byhead, jax.ShapeDtypeStruct((model, tokens), BF16)),
        in_specs=[anyspec] * 5,
        out_specs=(anyspec,) * 5,
        scratch_shapes=[
            pltpu.VMEM((model, total), BF16),
            pltpu.VMEM((tokens, model), BF16),
            pltpu.VMEM((n, tokens, hc), BF16),
            pltpu.VMEM((model, tokens), BF16),
            dma((4, n)),
            dma((4, n)),
            dma((7,)),
        ],
        compiler_params=pltpu.CompilerParams(
            collective_id=0, has_side_effects=True, vmem_limit_bytes=VMEM_BYTES
        ),
    )(queries[0], keys[0], values[0], out_weight, out_cot[0])

    block = pl.BlockSpec((BLOCK_TOKENS, hc), lambda i, picks: (i, 0))
    whole = pl.BlockSpec((length, hc), lambda i, picks: (0, 0))
    attn, dqh, dkh, dvh = pl.pallas_call(
        functools.partial(attention_kernel, heads, chosen, 1.0 / math.sqrt(HEAD_SIZE)),
        out_shape=(byhead,) * 4,
        grid_spec=pltpu.PrefetchScalarGridSpec(
            num_scalar_prefetch=1,
            grid=(blocks,),
            in_specs=[block, block, whole, whole],
            out_specs=(block, block, whole, whole),
            scratch_shapes=[
                pltpu.VMEM((heads, blocks, HEAD_SIZE, BLOCK_TOKENS), BF16),
                pltpu.VMEM((heads, blocks, HEAD_SIZE, BLOCK_TOKENS), BF16),
                pltpu.VMEM((heads, blocks, BLOCK_TOKENS, HEAD_SIZE), F32),
                pltpu.VMEM((heads, blocks, BLOCK_TOKENS, HEAD_SIZE), F32),
            ],
        ),
        compiler_params=pltpu.CompilerParams(vmem_limit_bytes=VMEM_BYTES),
    )(block_list, qh, ch, kh, vh)

    lane = (nz, n, sub, total)
    out, dq, dk, dv, wg = pl.pallas_call(
        functools.partial(scatter_kernel, n, nz),
        out_shape=(
            jax.ShapeDtypeStruct((tokens, model), BF16),
            bytoken,
            bytoken,
            bytoken,
            jax.ShapeDtypeStruct((sub, total), F32),
        ),
        in_specs=[anyspec] * 6,
        out_specs=(vspec, anyspec, anyspec, anyspec, vspec),
        scratch_shapes=[
            pltpu.VMEM((tokens, total), BF16),
            pltpu.VMEM((model, total), BF16),
            pltpu.VMEM((model, tokens), BF16),
            pltpu.VMEM(lane, F32),
            pltpu.VMEM(lane, BF16),
            pltpu.VMEM(lane, BF16),
            pltpu.VMEM(lane, BF16),
            pltpu.VMEM(lane, BF16),
            pltpu.VMEM(lane, BF16),
            pltpu.VMEM(lane[1:], BF16),
            pltpu.VMEM(lane[1:], BF16),
            dma((4, n)),
            dma((4, n)),
            dma((6,)),
            dma((nz,)),
            dma((nz,)),
            dma((nz, n)),
            dma((nz, n)),
            dma((nz, n)),
            dma((n,)),
            dma((n,)),
        ],
        compiler_params=pltpu.CompilerParams(
            collective_id=1, has_side_effects=True, vmem_limit_bytes=VMEM_BYTES
        ),
    )(attn, dqh, dkh, dvh, out_weight, oct_)
    return out[None], dq[None], dk[None], dv[None], wg


def solution(mesh):
    part = P("dp", "ctx", None)
    return jax.shard_map(
        shards,
        mesh=mesh,
        in_specs=(part, part, part, P(), part, P()),
        out_specs=(part, part, part, part, P(("dp", "ctx"), None)),
        check_vma=False,
    )
```

```python
import functools
import math

import jax
import jax.numpy as jnp
from jax import lax
from jax.experimental import pallas as pl
from jax.experimental.pallas import tpu as pltpu
from jax.sharding import PartitionSpec as P

HEAD_SIZE = 128
BLOCK_TOKENS = 128
MESH = pl.DeviceIdType.MESH
BF16 = jnp.bfloat16
F32 = jnp.float32
VMEM_BYTES = 60 * 1024 * 1024


def mm(a, b, ca=1, cb=0):
    return lax.dot_general(a, b, (((ca,), (cb,)), ((), ())), preferred_element_type=F32)


def span(i, size):
    return pl.ds(pl.multiple_of(i * size, size), size)


def layer_kernel(n, nz, heads, names, picks, pos, q, k, v, w, oc, out, dqo, dko, dvo, wg, *scratch):
    r = dict(zip(names, scratch))
    me = lax.axis_index("ctx")
    dp = lax.axis_index("dp")
    core = lax.rem(dp, 2)
    other = dp + 1 - 2 * core
    z = dp // 2
    held = q.shape[0]
    tokens = held * BLOCK_TOKENS
    model = w.shape[0]
    blocks, chosen = picks.shape
    sub = wg.shape[0]
    scale = 1.0 / math.sqrt(HEAD_SIZE)
    factor = scale * math.log2(math.e)
    ocv, octv, wv, seq = r["ocv"], r["octv"], r["wv"], r["seq"]
    acc, ps, dss, kt, vt = r["acc"], r["ps"], r["dss"], r["kt"], r["vt"]
    loc = r["loc"]

    barrier = pltpu.get_barrier_semaphore()
    up = lax.rem(z + 1, nz) * 2 + core
    down = lax.rem(z + nz - 1, nz) * 2 + core
    for d in range(1, n):
        pl.semaphore_signal(
            barrier, inc=1, device_id=(dp, lax.rem(me + d, n)), device_id_type=MESH
        )
    for target in (other, up, down):
        pl.semaphore_signal(barrier, inc=1, device_id=(target, me), device_id_type=MESH)
    load_oc = pltpu.make_async_copy(oc, ocv, loc.at[0])
    load_oc.start()
    load_w = []
    for h in range(heads):
        for p in range(n):
            copy = pltpu.make_async_copy(
                w.at[:, pl.ds((p * heads + h) * HEAD_SIZE, HEAD_SIZE)],
                wv.at[h, :, pl.ds(p * HEAD_SIZE, HEAD_SIZE)],
                r["wsem"].at[h, p],
            )
            copy.start()
            load_w.append(copy)
    pl.semaphore_wait(barrier, n - 1 + 3)

    def trade(src_of, dst, send, recv, own_sem):
        remote = []
        for d in range(1, n):
            p = lax.rem(me + d, n)
            copy = pltpu.make_async_remote_copy(
                src_of(p, d), dst, send.at[d], recv.at[d],
                device_id=(dp, p), device_id_type=MESH,
            )
            copy.start()
            remote.append(copy)
        own = pltpu.make_async_copy(src_of(me, 0), dst, own_sem)
        own.start()
        return own, remote

    def column(p, h):
        return span(p * heads + h, HEAD_SIZE)

    mine = pl.ds(me * held, held)

    def send_rows(h):
        return [
            trade(
                lambda p, d, x=x: x.at[:, :, column(p, h)], r[f"{t}{h}"].at[mine],
                r["in_s"].at[h, i], r["in_r"].at[h, i], r["in_l"].at[h, i],
            )
            for i, (t, x) in enumerate((("q", q), ("k", k), ("v", v)))
        ]

    def send_cot(h):
        return [
            trade(
                lambda p, d: r["cotbuf"].at[h, d], r[f"c{h}"].at[mine],
                r["in_s"].at[h, 3], r["in_r"].at[h, 3], r["in_l"].at[h, 3],
            )
        ]

    def work_cot(h):
        for d in range(n):
            p = lax.rem(me + d, n)
            r["cotbuf"][h, d] = (
                mm(ocv[...], wv[h, :, span(p, HEAD_SIZE)])
                .astype(BF16)
                .reshape(held, BLOCK_TOKENS, HEAD_SIZE)
            )

    sent = []

    def arrive(trades):
        for own, remote in trades:
            own.wait()
            for copy in remote:
                copy.wait_recv()
            sent.extend(remote)

    coming = send_rows(0)
    load_oc.wait()
    for copy in load_w:
        copy.wait()
    work_cot(0)
    coming += send_cot(0)
    for h in range(1, heads):
        work_cot(h)

    def flip(i, carry):
        octv[span(i, 256), :] = ocv[:, span(i, 256)].T
        return carry

    lax.fori_loop(0, model // 256, flip, 0)

    def clear(i, carry):
        ps[i, chosen] = jnp.zeros((BLOCK_TOKENS, BLOCK_TOKENS), BF16)
        dss[i, chosen] = jnp.zeros((BLOCK_TOKENS, BLOCK_TOKENS), BF16)
        return carry

    lax.fori_loop(0, blocks, clear, 0)

    def attend(h, i):
        at = span(i, BLOCK_TOKENS)
        kh, vh = r[f"k{h}"], r[f"v{h}"]
        qi = r[f"q{h}"][i]
        ci = r[f"c{h}"][i]
        ids = [picks[i, j] for j in range(chosen)]
        ks = jnp.concatenate([kh[b] for b in ids], axis=0)
        vs = jnp.concatenate([vh[b] for b in ids], axis=0)
        kts = jnp.concatenate([kt[b] for b in ids], axis=1)
        vts = jnp.concatenate([vt[b] for b in ids], axis=1)
        st = mm(ks, qi, 1, 1)
        dpt = mm(vs, ci, 1, 1)
        top = jnp.max(st, axis=0, keepdims=True)
        e = jnp.exp2((st - top) * factor)
        inv = 1.0 / jnp.sum(e, axis=0, keepdims=True)
        pt = e * inv
        low = pt.astype(BF16)
        a = mm(vts, low).astype(BF16)
        r["attn"][h, at, :] = a.T
        dot = jnp.sum(ci.astype(F32).T * a.astype(F32), axis=0, keepdims=True)
        ds = (pt * (dpt - dot)).astype(BF16)
        r["dq"][h, at, :] = (mm(kts, ds) * scale).T.astype(BF16)
        for j in range(chosen):
            part = slice(j * BLOCK_TOKENS, (j + 1) * BLOCK_TOKENS)
            ps[i, j] = low[part]
            dss[i, j] = ds[part]

    def collect(h):
        def body(j, carry):
            at = span(j, BLOCK_TOKENS)
            slots = [pos[i, j] for i in range(blocks)]
            dst = jnp.concatenate([dss[i, s] for i, s in enumerate(slots)], axis=1)
            r["dk"][h, at, :] = (mm(dst, r[f"q{h}"][...].reshape(-1, HEAD_SIZE)) * scale).astype(BF16)
            pst = jnp.concatenate([ps[i, s] for i, s in enumerate(slots)], axis=1)
            r["dv"][h, at, :] = mm(pst, r[f"c{h}"][...].reshape(-1, HEAD_SIZE)).astype(BF16)
            return carry

        lax.fori_loop(0, blocks, body, 0)

    def turn(h):
        def body(b, carry):
            kt[b] = r[f"k{h}"][b].T
            vt[b] = r[f"v{h}"][b].T
            return carry

        lax.fori_loop(0, blocks, body, 0)

    def send_attn(h):
        return [
            trade(
                lambda p, d: r["attn"].at[h, span(p, tokens), :],
                seq.at[h, :, span(me, HEAD_SIZE)],
                r["out_s"].at[h, 0], r["out_r"].at[h, 0], r["out_l"].at[h, 0],
            )
        ]

    def send_grads(h):
        return [
            trade(
                lambda p, d, t=t: r[t].at[h, span(p, tokens), :], o.at[:, column(me, h)],
                r["out_s"].at[h, i], r["out_r"].at[h, i], r["out_l"].at[h, i],
            )
            for i, t, o in ((1, "dq", dqo), (2, "dk", dko), (3, "dv", dvo))
        ]

    def term(h, c, s, who):
        return mm(octv[span((2 * c + who) * n + s, sub), :], seq[h])

    def core_copy(h, c):
        return pltpu.make_async_remote_copy(
            r["csend"].at[h, c], r["crecv"].at[h, c], r["csem_s"].at[h, c], r["csem_r"].at[h, c],
            device_id=(other, me), device_id_type=MESH,
        )

    def give(h):
        def body(c, carry):
            for s in range(n):
                r["csend"][h, c, s] = term(h, c, s, 1 - core).astype(BF16)
            core_copy(h, c).start()
            return carry

        lax.fori_loop(0, nz, body, 0)

        def keep(c, carry):
            for s in range(n):
                acc[h, c, s] = term(h, c, s, core)
            return carry

        lax.fori_loop(0, nz, keep, 0)

    def take(h):
        def body(c, carry):
            core_copy(h, c).wait()
            for s in range(n):
                acc[h, c, s] += r["crecv"][h, c, s].astype(F32)
            return carry

        lax.fori_loop(0, nz, body, 0)

    def hop(h, c, s, buf, sem, target):
        return pltpu.make_async_remote_copy(
            r["zsend"].at[h, c, s], r[buf].at[h, c, s], r["zsem"].at[h, c, s],
            r[sem].at[h, c, s], device_id=(target, me), device_id_type=MESH,
        )

    def right(h, c, s):
        return hop(h, c, s, "rrecv", "rsem", up)

    def left(h, c, s):
        return hop(h, c, s, "lrecv", "lsem", down)

    def line(h, u):
        i = u - z

        @pl.when((i >= 0) & (i < (nz - 1 - z) * n))
        def _():
            c = nz - 1 - i // n
            s = lax.rem(i, n)

            @pl.when(z > 0)
            def _():
                right(h, c, s).wait_recv()
                acc[h, c, s] += r["rrecv"][h, c, s].astype(F32)

            r["zsend"][h, c, s] = acc[h, c, s].astype(BF16)
            right(h, c, s).start()

        j = u - (nz - 1 - z)

        @pl.when((j >= 0) & (j < z * n))
        def _():
            c = j // n
            s = lax.rem(j, n)

            @pl.when(z < nz - 1)
            def _():
                left(h, c, s).wait_recv()
                acc[h, c, s] += r["lrecv"][h, c, s].astype(F32)

            r["zsend"][h, c, s] = acc[h, c, s].astype(BF16)
            left(h, c, s).start()

    hops = (nz - 1) * n + nz

    def lines(h, first):
        def body(u, carry):
            line(h, u)
            return carry

        lax.fori_loop(first, hops, body, 0)

    def cross(h, s, slot):
        return pltpu.make_async_remote_copy(
            r["xsend"].at[h, s], r["xrecv"].at[h, slot], r["xsem_s"].at[h, s],
            r["xsem_r"].at[h, slot], device_id=(dp, s), device_id_type=MESH,
        )

    def finish(h):
        def body(s, carry):
            @pl.when(z > 0)
            def _():
                right(h, z, s).wait_recv()
                acc[h, z, s] += r["rrecv"][h, z, s].astype(F32)

            @pl.when(z < nz - 1)
            def _():
                left(h, z, s).wait_recv()
                acc[h, z, s] += r["lrecv"][h, z, s].astype(F32)

            @pl.when(s != me)
            def _():
                r["xsend"][h, s] = acc[h, z, s].astype(BF16)
                cross(h, s, me).start()

            return carry

        lax.fori_loop(0, n, body, 0)

    def total(h):
        r["sum"][...] = acc[h, z, me]

        def body(p, carry):
            @pl.when(p != me)
            def _():
                cross(h, p, p).wait_recv()
                r["sum"][...] += r["xrecv"][h, p].astype(F32)

            return carry

        lax.fori_loop(0, n, body, 0)
        for p in range(n):
            wg[:, pl.ds((p * heads + h) * HEAD_SIZE, HEAD_SIZE)] = r["sum"][
                :, p * HEAD_SIZE : (p + 1) * HEAD_SIZE
            ] * (1.0 / (2 * nz))

    def drain(h):
        def body(s, carry):
            @pl.when(s != me)
            def _():
                cross(h, s, me).wait_send()

            for c in range(nz):
                @pl.when(z < c)
                def _():
                    right(h, c, s).wait_send()

                @pl.when(z > c)
                def _():
                    left(h, c, s).wait_send()

            return carry

        lax.fori_loop(0, n, body, 0)

    pair = math.gcd(blocks, 2)
    turns = blocks // pair
    begin = turns // 2
    per = 3
    done = min(hops, (turns - begin) * per)
    going, attn_going = [], []
    for h in range(heads):
        arrive(coming)
        if h + 1 < heads:
            coming = send_rows(h + 1) + send_cot(h + 1)
        turn(h)

        def body(t, carry, h=h):
            for b in range(pair):
                attend(h, t * pair + b)
            if h > 0:
                @pl.when(t == begin - 1)
                def _():
                    give(h - 1)

                @pl.when(t == begin)
                def _():
                    take(h - 1)

                @pl.when(t >= begin)
                def _():
                    for x in range(per):
                        line(h - 1, (t - begin) * per + x)

            return carry

        if h > 0:
            split = min(begin - 1, 2)
            lax.fori_loop(0, split, body, 0)
            arrive(attn_going)
            lax.fori_loop(split, turns, body, 0)
        else:
            lax.fori_loop(0, turns, body, 0)
        attn_going = send_attn(h)
        collect(h)
        if h > 0:
            lines(h - 1, done)
            finish(h - 1)
        if h + 1 < heads:
            going += send_grads(h)
    arrive(attn_going)
    going += send_grads(heads - 1)
    give(heads - 1)
    tile = 256

    def project(i, carry):
        at = span(i, tile)
        part = mm(seq[0], wv[0, at, :], 1, 1)
        for h in range(1, heads):
            part += mm(seq[h], wv[h, at, :], 1, 1)
        out[:, at] = part.astype(BF16)
        return carry

    take(heads - 1)

    def both(u, carry):
        line(heads - 1, u)

        @pl.when(u < model // tile)
        def _():
            project(u, 0)

        return carry

    lax.fori_loop(0, max(hops, model // tile), both, 0)
    finish(heads - 1)
    for h in range(heads):
        total(h)
    for h in range(heads):
        drain(h)
    arrive(going)
    for copy in sent:
        copy.wait_send()


def shards(queries, keys, values, out_weight, out_cot, block_list):
    n = lax.axis_size("ctx")
    n_dp = lax.axis_size("dp")
    nz = n_dp // 2
    _, tokens, total = queries.shape
    model = out_weight.shape[0]
    heads = total // n // HEAD_SIZE
    length = tokens * n
    held = tokens // BLOCK_TOKENS
    blocks, chosen = block_list.shape
    sub = model // (n * n_dp)
    anyspec = pl.BlockSpec(memory_space=pl.ANY)
    vspec = pl.BlockSpec(memory_space=pltpu.VMEM)
    sspec = pl.BlockSpec(memory_space=pltpu.SMEM)
    dma = pltpu.SemaphoreType.DMA

    listed = block_list[:, :, None] == jnp.arange(blocks, dtype=jnp.int32)
    slot = jnp.arange(chosen, dtype=jnp.int32)[None, :, None] - chosen
    pos = chosen + jnp.sum(jnp.where(listed, slot, 0), axis=1)

    width = n * HEAD_SIZE
    lane = (heads, nz, n, sub, width)
    cross = (heads, n, sub, width)
    byhead = (heads, length, HEAD_SIZE)
    scratch = {
        "ocv": pltpu.VMEM((tokens, model), BF16),
        "octv": pltpu.VMEM((model, tokens), BF16),
        "wv": pltpu.VMEM((heads, model, width), BF16),
        "seq": pltpu.VMEM((heads, tokens, width), BF16),
        "cotbuf": pltpu.VMEM((heads, n, held, BLOCK_TOKENS, HEAD_SIZE), BF16),
        "attn": pltpu.VMEM(byhead, BF16),
        "dq": pltpu.VMEM(byhead, BF16),
        "dk": pltpu.VMEM(byhead, BF16),
        "dv": pltpu.VMEM(byhead, BF16),
        "ps": pltpu.VMEM((blocks, chosen + 1, BLOCK_TOKENS, BLOCK_TOKENS), BF16),
        "dss": pltpu.VMEM((blocks, chosen + 1, BLOCK_TOKENS, BLOCK_TOKENS), BF16),
        "kt": pltpu.VMEM((blocks, HEAD_SIZE, BLOCK_TOKENS), BF16),
        "vt": pltpu.VMEM((blocks, HEAD_SIZE, BLOCK_TOKENS), BF16),
        "acc": pltpu.VMEM(lane, F32),
        "sum": pltpu.VMEM((sub, width), F32),
        "csend": pltpu.VMEM(lane, BF16),
        "crecv": pltpu.VMEM(lane, BF16),
        "zsend": pltpu.VMEM(lane, BF16),
        "rrecv": pltpu.VMEM(lane, BF16),
        "lrecv": pltpu.VMEM(lane, BF16),
        "xsend": pltpu.VMEM(cross, BF16),
        "xrecv": pltpu.VMEM(cross, BF16),
        "loc": dma((1,)),
        "wsem": dma((heads, n)),
        "in_s": dma((heads, 4, n)),
        "in_r": dma((heads, 4, n)),
        "in_l": dma((heads, 4)),
        "out_s": dma((heads, 4, n)),
        "out_r": dma((heads, 4, n)),
        "out_l": dma((heads, 4)),
        "csem_s": dma((heads, nz)),
        "csem_r": dma((heads, nz)),
        "zsem": dma((heads, nz, n)),
        "rsem": dma((heads, nz, n)),
        "lsem": dma((heads, nz, n)),
        "xsem_s": dma((heads, n)),
        "xsem_r": dma((heads, n)),
    }
    for h in range(heads):
        for t in "qkvc":
            scratch[f"{t}{h}"] = pltpu.VMEM((blocks, BLOCK_TOKENS, HEAD_SIZE), BF16)
    rows = [x.reshape(held, BLOCK_TOKENS, total) for x in (queries, keys, values)]
    bytoken = jax.ShapeDtypeStruct((tokens, total), BF16)
    out, dq, dk, dv, wg = pl.pallas_call(
        functools.partial(layer_kernel, n, nz, heads, tuple(scratch)),
        out_shape=(
            jax.ShapeDtypeStruct((tokens, model), BF16),
            bytoken,
            bytoken,
            bytoken,
            jax.ShapeDtypeStruct((sub, total), F32),
        ),
        in_specs=[sspec] * 2 + [anyspec] * 5,
        out_specs=(vspec, anyspec, anyspec, anyspec, vspec),
        scratch_shapes=list(scratch.values()),
        compiler_params=pltpu.CompilerParams(
            collective_id=0, has_side_effects=True, vmem_limit_bytes=VMEM_BYTES
        ),
    )(block_list, pos, *rows, out_weight, out_cot[0])
    return out[None], dq[None], dk[None], dv[None], wg


def solution(mesh):
    part = P("dp", "ctx", None)
    return jax.shard_map(
        shards,
        mesh=mesh,
        in_specs=(part, part, part, P(), part, P()),
        out_specs=(part, part, part, part, P(("dp", "ctx"), None)),
        check_vma=False,
    )
```

```python
import functools
import math

import jax
import jax.numpy as jnp
from jax import lax
from jax.experimental import pallas as pl
from jax.experimental.pallas import tpu as pltpu
from jax.sharding import PartitionSpec as P

HEAD_SIZE = 128
BLOCK_TOKENS = 128
MESH = pl.DeviceIdType.MESH
BF16 = jnp.bfloat16
F32 = jnp.float32
VMEM_BYTES = 60 * 1024 * 1024


def mm(a, b, ca=1, cb=0):
    return lax.dot_general(a, b, (((ca,), (cb,)), ((), ())), preferred_element_type=F32)


def span(i, size):
    return pl.ds(pl.multiple_of(i * size, size), size)


def layer_kernel(n, nz, heads, names, picks, pos, q, k, v, w, oc, out, dqo, dko, dvo, wg, *scratch):
    r = dict(zip(names, scratch))
    me = lax.axis_index("ctx")
    dp = lax.axis_index("dp")
    core = lax.rem(dp, 2)
    other = dp + 1 - 2 * core
    z = dp // 2
    held = q.shape[0]
    tokens = held * BLOCK_TOKENS
    model = w.shape[0]
    blocks, chosen = picks.shape
    sub = wg.shape[0]
    scale = 1.0 / math.sqrt(HEAD_SIZE)
    factor = scale * math.log2(math.e)
    ocv, octv, wv, seq = r["ocv"], r["octv"], r["wv"], r["seq"]
    acc, ps, dss, kt, vt = r["acc"], r["ps"], r["dss"], r["kt"], r["vt"]
    loc = r["loc"]

    barrier = pltpu.get_barrier_semaphore()
    up = lax.rem(z + 1, nz) * 2 + core
    down = lax.rem(z + nz - 1, nz) * 2 + core
    for d in range(1, n):
        pl.semaphore_signal(
            barrier, inc=1, device_id=(dp, lax.rem(me + d, n)), device_id_type=MESH
        )
    for target in (other, up, down):
        pl.semaphore_signal(barrier, inc=1, device_id=(target, me), device_id_type=MESH)
    load_oc = pltpu.make_async_copy(oc, ocv, loc.at[0])
    load_oc.start()
    load_w = []
    for h in range(heads):
        for p in range(n):
            copy = pltpu.make_async_copy(
                w.at[:, pl.ds((p * heads + h) * HEAD_SIZE, HEAD_SIZE)],
                wv.at[h, :, pl.ds(p * HEAD_SIZE, HEAD_SIZE)],
                r["wsem"].at[h, p],
            )
            copy.start()
            load_w.append(copy)
    pl.semaphore_wait(barrier, n - 1 + 3)

    def trade(src_of, dst, send, recv, own_sem):
        remote = []
        for d in range(1, n):
            p = lax.rem(me + d, n)
            copy = pltpu.make_async_remote_copy(
                src_of(p, d), dst, send.at[d], recv.at[d],
                device_id=(dp, p), device_id_type=MESH,
            )
            copy.start()
            remote.append(copy)
        own = pltpu.make_async_copy(src_of(me, 0), dst, own_sem)
        own.start()
        return own, remote

    def column(p, h):
        return span(p * heads + h, HEAD_SIZE)

    mine = pl.ds(me * held, held)

    def send_rows(h):
        return [
            trade(
                lambda p, d, x=x: x.at[:, :, column(p, h)], r[f"{t}{h}"].at[mine],
                r["in_s"].at[h, i], r["in_r"].at[h, i], r["in_l"].at[h, i],
            )
            for i, (t, x) in enumerate((("q", q), ("k", k), ("v", v)))
        ]

    def send_cot(h):
        return [
            trade(
                lambda p, d: r["cotbuf"].at[h, d], r[f"c{h}"].at[mine],
                r["in_s"].at[h, 3], r["in_r"].at[h, 3], r["in_l"].at[h, 3],
            )
        ]

    def work_cot(h):
        for d in range(n):
            p = lax.rem(me + d, n)
            r["cotbuf"][h, d] = (
                mm(ocv[...], wv[h, :, span(p, HEAD_SIZE)])
                .astype(BF16)
                .reshape(held, BLOCK_TOKENS, HEAD_SIZE)
            )

    sent = []

    def arrive(trades):
        for own, remote in trades:
            own.wait()
            for copy in remote:
                copy.wait_recv()
            sent.extend(remote)

    coming = send_rows(0)
    load_oc.wait()
    for copy in load_w:
        copy.wait()
    work_cot(0)
    coming += send_cot(0)
    for h in range(1, heads):
        work_cot(h)

    def flip(i, carry):
        octv[span(i, 256), :] = ocv[:, span(i, 256)].T
        return carry

    lax.fori_loop(0, model // 256, flip, 0)

    def clear(i, carry):
        ps[i, chosen] = jnp.zeros((BLOCK_TOKENS, BLOCK_TOKENS), BF16)
        dss[i, chosen] = jnp.zeros((BLOCK_TOKENS, BLOCK_TOKENS), BF16)
        return carry

    lax.fori_loop(0, blocks, clear, 0)

    def attend(h, i):
        at = span(i, BLOCK_TOKENS)
        kh, vh = r[f"k{h}"], r[f"v{h}"]
        qi = r[f"q{h}"][i]
        ci = r[f"c{h}"][i]
        ids = [picks[i, j] for j in range(chosen)]
        ks = jnp.concatenate([kh[b] for b in ids], axis=0)
        vs = jnp.concatenate([vh[b] for b in ids], axis=0)
        kts = jnp.concatenate([kt[b] for b in ids], axis=1)
        vts = jnp.concatenate([vt[b] for b in ids], axis=1)
        st = mm(ks, qi, 1, 1)
        dpt = mm(vs, ci, 1, 1)
        top = jnp.max(st, axis=0, keepdims=True)
        e = jnp.exp2((st - top) * factor)
        inv = 1.0 / jnp.sum(e, axis=0, keepdims=True)
        pt = e * inv
        low = pt.astype(BF16)
        a = mm(vts, low).astype(BF16)
        r["attn"][h, at, :] = a.T
        dot = jnp.sum(ci.astype(F32).T * a.astype(F32), axis=0, keepdims=True)
        ds = (pt * (dpt - dot)).astype(BF16)
        r["dq"][h, at, :] = (mm(kts, ds) * scale).T.astype(BF16)
        for j in range(chosen):
            part = slice(j * BLOCK_TOKENS, (j + 1) * BLOCK_TOKENS)
            ps[i, j] = low[part]
            dss[i, j] = ds[part]

    group = math.gcd(blocks, 4)

    def collect(h):
        def wide(kept, g):
            return jnp.concatenate(
                [
                    jnp.concatenate([kept[i, pos[i, g * group + x]] for i in range(blocks)], axis=1)
                    for x in range(group)
                ],
                axis=0,
            )

        def body(g, carry):
            at = span(g, group * BLOCK_TOKENS)
            dst = wide(dss, g)
            r["dk"][h, at, :] = (mm(dst, r[f"q{h}"][...].reshape(-1, HEAD_SIZE)) * scale).astype(BF16)
            pst = wide(ps, g)
            r["dv"][h, at, :] = mm(pst, r[f"c{h}"][...].reshape(-1, HEAD_SIZE)).astype(BF16)
            return carry

        lax.fori_loop(0, blocks // group, body, 0)

    def turn(h):
        def body(b, carry):
            kt[b] = r[f"k{h}"][b].T
            vt[b] = r[f"v{h}"][b].T
            return carry

        lax.fori_loop(0, blocks, body, 0)

    def send_attn(h):
        return [
            trade(
                lambda p, d: r["attn"].at[h, span(p, tokens), :],
                seq.at[h, :, span(me, HEAD_SIZE)],
                r["out_s"].at[h, 0], r["out_r"].at[h, 0], r["out_l"].at[h, 0],
            )
        ]

    def send_grads(h):
        return [
            trade(
                lambda p, d, t=t: r[t].at[h, span(p, tokens), :], o.at[:, column(me, h)],
                r["out_s"].at[h, i], r["out_r"].at[h, i], r["out_l"].at[h, i],
            )
            for i, t, o in ((1, "dq", dqo), (2, "dk", dko), (3, "dv", dvo))
        ]

    def term(h, c, who):
        return mm(octv[span(2 * c + who, n * sub), :], seq[h]).reshape(n, sub, -1)

    def core_copy(h, c):
        return pltpu.make_async_remote_copy(
            r["csend"].at[h, c], r["crecv"].at[h, c], r["csem_s"].at[h, c], r["csem_r"].at[h, c],
            device_id=(other, me), device_id_type=MESH,
        )

    def give(h):
        def body(c, carry):
            r["csend"][h, c] = term(h, c, 1 - core).astype(BF16)
            core_copy(h, c).start()
            return carry

        lax.fori_loop(0, nz, body, 0)

        def keep(c, carry):
            acc[h, c] = term(h, c, core)
            return carry

        lax.fori_loop(0, nz, keep, 0)

    def take(h):
        def body(c, carry):
            core_copy(h, c).wait()
            for s in range(n):
                acc[h, c, s] += r["crecv"][h, c, s].astype(F32)
            return carry

        lax.fori_loop(0, nz, body, 0)

    def hop(h, c, s, buf, sem, target):
        return pltpu.make_async_remote_copy(
            r["zsend"].at[h, c, s], r[buf].at[h, c, s], r["zsem"].at[h, c, s],
            r[sem].at[h, c, s], device_id=(target, me), device_id_type=MESH,
        )

    def right(h, c, s):
        return hop(h, c, s, "rrecv", "rsem", up)

    def left(h, c, s):
        return hop(h, c, s, "lrecv", "lsem", down)

    def line(h, u):
        i = u - z

        @pl.when((i >= 0) & (i < (nz - 1 - z) * n))
        def _():
            c = nz - 1 - i // n
            s = lax.rem(i, n)

            @pl.when(z > 0)
            def _():
                right(h, c, s).wait_recv()
                acc[h, c, s] += r["rrecv"][h, c, s].astype(F32)

            r["zsend"][h, c, s] = acc[h, c, s].astype(BF16)
            right(h, c, s).start()

        j = u - (nz - 1 - z)

        @pl.when((j >= 0) & (j < z * n))
        def _():
            c = j // n
            s = lax.rem(j, n)

            @pl.when(z < nz - 1)
            def _():
                left(h, c, s).wait_recv()
                acc[h, c, s] += r["lrecv"][h, c, s].astype(F32)

            r["zsend"][h, c, s] = acc[h, c, s].astype(BF16)
            left(h, c, s).start()

    hops = (nz - 1) * n + nz

    def lines(h, first):
        def body(u, carry):
            line(h, u)
            return carry

        lax.fori_loop(first, hops, body, 0)

    def cross(h, s, slot):
        return pltpu.make_async_remote_copy(
            r["xsend"].at[h, s], r["xrecv"].at[h, slot], r["xsem_s"].at[h, s],
            r["xsem_r"].at[h, slot], device_id=(dp, s), device_id_type=MESH,
        )

    def finish(h):
        def body(s, carry):
            @pl.when(z > 0)
            def _():
                right(h, z, s).wait_recv()
                acc[h, z, s] += r["rrecv"][h, z, s].astype(F32)

            @pl.when(z < nz - 1)
            def _():
                left(h, z, s).wait_recv()
                acc[h, z, s] += r["lrecv"][h, z, s].astype(F32)

            @pl.when(s != me)
            def _():
                r["xsend"][h, s] = acc[h, z, s].astype(BF16)
                cross(h, s, me).start()

            return carry

        lax.fori_loop(0, n, body, 0)

    def total(h):
        r["sum"][...] = acc[h, z, me]

        def body(p, carry):
            @pl.when(p != me)
            def _():
                cross(h, p, p).wait_recv()
                r["sum"][...] += r["xrecv"][h, p].astype(F32)

            return carry

        lax.fori_loop(0, n, body, 0)
        for p in range(n):
            wg[:, pl.ds((p * heads + h) * HEAD_SIZE, HEAD_SIZE)] = r["sum"][
                :, p * HEAD_SIZE : (p + 1) * HEAD_SIZE
            ] * (1.0 / (2 * nz))

    def drain(h):
        def body(s, carry):
            @pl.when(s != me)
            def _():
                cross(h, s, me).wait_send()

            for c in range(nz):
                @pl.when(z < c)
                def _():
                    right(h, c, s).wait_send()

                @pl.when(z > c)
                def _():
                    left(h, c, s).wait_send()

            return carry

        lax.fori_loop(0, n, body, 0)

    pair = math.gcd(blocks, 2)
    turns = blocks // pair
    begin = turns // 2
    per = 3
    done = min(hops, (turns - begin) * per)
    going, attn_going = [], []
    for h in range(heads):
        arrive(coming)
        if h + 1 < heads:
            coming = send_rows(h + 1) + send_cot(h + 1)
        turn(h)

        def body(t, carry, h=h):
            for b in range(pair):
                attend(h, t * pair + b)
            if h > 0:
                @pl.when(t == begin - 1)
                def _():
                    give(h - 1)

                @pl.when(t == begin)
                def _():
                    take(h - 1)

                @pl.when(t >= begin)
                def _():
                    for x in range(per):
                        line(h - 1, (t - begin) * per + x)

            return carry

        if h > 0:
            split = min(begin - 1, 2)
            lax.fori_loop(0, split, body, 0)
            arrive(attn_going)
            lax.fori_loop(split, turns, body, 0)
        else:
            lax.fori_loop(0, turns, body, 0)
        attn_going = send_attn(h)
        collect(h)
        if h > 0:
            lines(h - 1, done)
            finish(h - 1)
        if h + 1 < heads:
            going += send_grads(h)
    arrive(attn_going)
    going += send_grads(heads - 1)
    give(heads - 1)
    tile = 256

    def project(i, carry):
        at = span(i, tile)
        part = mm(seq[0], wv[0, at, :], 1, 1)
        for h in range(1, heads):
            part += mm(seq[h], wv[h, at, :], 1, 1)
        out[:, at] = part.astype(BF16)
        return carry

    take(heads - 1)

    def both(u, carry):
        line(heads - 1, u)

        @pl.when(u < model // tile)
        def _():
            project(u, 0)

        return carry

    lax.fori_loop(0, max(hops, model // tile), both, 0)
    finish(heads - 1)
    for h in range(heads):
        total(h)
    for h in range(heads):
        drain(h)
    arrive(going)
    for copy in sent:
        copy.wait_send()


def shards(queries, keys, values, out_weight, out_cot, block_list):
    n = lax.axis_size("ctx")
    n_dp = lax.axis_size("dp")
    nz = n_dp // 2
    _, tokens, total = queries.shape
    model = out_weight.shape[0]
    heads = total // n // HEAD_SIZE
    length = tokens * n
    held = tokens // BLOCK_TOKENS
    blocks, chosen = block_list.shape
    sub = model // (n * n_dp)
    anyspec = pl.BlockSpec(memory_space=pl.ANY)
    vspec = pl.BlockSpec(memory_space=pltpu.VMEM)
    sspec = pl.BlockSpec(memory_space=pltpu.SMEM)
    dma = pltpu.SemaphoreType.DMA

    listed = block_list[:, :, None] == jnp.arange(blocks, dtype=jnp.int32)
    slot = jnp.arange(chosen, dtype=jnp.int32)[None, :, None] - chosen
    pos = chosen + jnp.sum(jnp.where(listed, slot, 0), axis=1)

    width = n * HEAD_SIZE
    lane = (heads, nz, n, sub, width)
    cross = (heads, n, sub, width)
    byhead = (heads, length, HEAD_SIZE)
    scratch = {
        "ocv": pltpu.VMEM((tokens, model), BF16),
        "octv": pltpu.VMEM((model, tokens), BF16),
        "wv": pltpu.VMEM((heads, model, width), BF16),
        "seq": pltpu.VMEM((heads, tokens, width), BF16),
        "cotbuf": pltpu.VMEM((heads, n, held, BLOCK_TOKENS, HEAD_SIZE), BF16),
        "attn": pltpu.VMEM(byhead, BF16),
        "dq": pltpu.VMEM(byhead, BF16),
        "dk": pltpu.VMEM(byhead, BF16),
        "dv": pltpu.VMEM(byhead, BF16),
        "ps": pltpu.VMEM((blocks, chosen + 1, BLOCK_TOKENS, BLOCK_TOKENS), BF16),
        "dss": pltpu.VMEM((blocks, chosen + 1, BLOCK_TOKENS, BLOCK_TOKENS), BF16),
        "kt": pltpu.VMEM((blocks, HEAD_SIZE, BLOCK_TOKENS), BF16),
        "vt": pltpu.VMEM((blocks, HEAD_SIZE, BLOCK_TOKENS), BF16),
        "acc": pltpu.VMEM(lane, F32),
        "sum": pltpu.VMEM((sub, width), F32),
        "csend": pltpu.VMEM(lane, BF16),
        "crecv": pltpu.VMEM(lane, BF16),
        "zsend": pltpu.VMEM(lane, BF16),
        "rrecv": pltpu.VMEM(lane, BF16),
        "lrecv": pltpu.VMEM(lane, BF16),
        "xsend": pltpu.VMEM(cross, BF16),
        "xrecv": pltpu.VMEM(cross, BF16),
        "loc": dma((1,)),
        "wsem": dma((heads, n)),
        "in_s": dma((heads, 4, n)),
        "in_r": dma((heads, 4, n)),
        "in_l": dma((heads, 4)),
        "out_s": dma((heads, 4, n)),
        "out_r": dma((heads, 4, n)),
        "out_l": dma((heads, 4)),
        "csem_s": dma((heads, nz)),
        "csem_r": dma((heads, nz)),
        "zsem": dma((heads, nz, n)),
        "rsem": dma((heads, nz, n)),
        "lsem": dma((heads, nz, n)),
        "xsem_s": dma((heads, n)),
        "xsem_r": dma((heads, n)),
    }
    for h in range(heads):
        for t in "qkvc":
            scratch[f"{t}{h}"] = pltpu.VMEM((blocks, BLOCK_TOKENS, HEAD_SIZE), BF16)
    rows = [x.reshape(held, BLOCK_TOKENS, total) for x in (queries, keys, values)]
    bytoken = jax.ShapeDtypeStruct((tokens, total), BF16)
    out, dq, dk, dv, wg = pl.pallas_call(
        functools.partial(layer_kernel, n, nz, heads, tuple(scratch)),
        out_shape=(
            jax.ShapeDtypeStruct((tokens, model), BF16),
            bytoken,
            bytoken,
            bytoken,
            jax.ShapeDtypeStruct((sub, total), F32),
        ),
        in_specs=[sspec] * 2 + [anyspec] * 5,
        out_specs=(vspec, anyspec, anyspec, anyspec, vspec),
        scratch_shapes=list(scratch.values()),
        compiler_params=pltpu.CompilerParams(
            collective_id=0, has_side_effects=True, vmem_limit_bytes=VMEM_BYTES
        ),
    )(block_list, pos, *rows, out_weight, out_cot[0])
    return out[None], dq[None], dk[None], dv[None], wg


def solution(mesh):
    part = P("dp", "ctx", None)
    return jax.shard_map(
        shards,
        mesh=mesh,
        in_specs=(part, part, part, P(), part, P()),
        out_specs=(part, part, part, part, P(("dp", "ctx"), None)),
        check_vma=False,
    )
```
